512 devices in a mesh: dp: 2 (over y_lo), tm: 256 (over y_hi, x, z, core).
Axes of the slice: x: 4, y: 4 (y_hi: 2, y_lo: 2; y = y_hi * 2 + y_lo), z: 16, core: 2. Of those that a mesh axis runs over, the one named last changes fastest.
Arguments:
- inputs: bfloat16 [2, 262144, 256], P('dp', 'tm'), may hold values from -6 to 6
- cotangent: bfloat16 [2, 262144, 256], P('dp', 'tm'), may hold values from -6 to 6
- first_filter_weight: bfloat16 [2, 256, 512], replicated, may hold values from -0.25 to 0.25
- first_residual_matrix: bfloat16 [256, 256], replicated, may hold values from -0.375 to 0.375
- second_filter_weight: bfloat16 [2, 256, 512], replicated, may hold values from -0.25 to 0.25
- second_residual_matrix: bfloat16 [256, 256], replicated, may hold values from -0.375 to 0.375
Outputs:
- gradient_by_input: bfloat16 [2, 262144, 256], P('dp', 'tm')
- grads_first: float32 [327680], P(('dp', 'tm'))
- grads_second: float32 [327680], P(('dp', 'tm'))
The draws below stay inside these ranges and needn't reach their ends.
All inputs are finite; a program needn't handle non-finite values.
Results may differ from the reference program's by a relative error of at most 0.008.
Values may be sent and summed in bfloat16 or wider, within the bound.
No kernel may reach another device: no remote copies, remote signals or barrier semaphores. Data moves between devices by JAX's collectives and lax.ppermute only.
A program may use at most 64 MiB of HBM per device.

```python
import jax
import jax.numpy as jnp
from jax import lax

RES = 256
GATE = 512
HALF = 256
L_DEV = 1024
STREAMS = 2
TLEN = 262144
SPACING_FIRST = 8192
SPACING_SECOND = 32768


def block_scale(key, dims, split, least, largest):
    loudness, own = 1.0, jax.random.fold_in(key, 6)
    for position, blocks in split:
        heights = jnp.exp(jax.random.uniform(jax.random.fold_in(own, position), (blocks,), jnp.float32, least / len(split), largest / len(split)))
        loudness = loudness * jnp.repeat(heights, dims[position] // blocks).reshape([-1 if axis == position else 1 for axis in range(len(dims))])
    return loudness


def scatter_about(own_key, shape, deviation, most, split=(), kind=jnp.bfloat16):
    level = block_scale(own_key, shape, split, -0.22, 0.18) if split else 1.0
    array = jax.random.normal(own_key, shape, jnp.float32) * deviation * level
    return jnp.minimum(jnp.maximum(array, -most), most).astype(kind)


def setup_inputs(seed: int = 0) -> dict:
    key_of = jax.random.split(jax.random.key(seed), 7)
    return {
        "inputs": scatter_about(key_of[0], (STREAMS, TLEN, RES), 1.0, 6.0, ((0, 2), (1, 256))),
        "cotangent": scatter_about(key_of[1], (STREAMS, TLEN, RES), 1.0, 6.0, ((0, 2), (1, 256))),
        "first_filter_weight": scatter_about(key_of[2], (2, RES, GATE), (2 * RES) ** -0.5, 0.25),
        "first_residual_matrix": scatter_about(key_of[3], (HALF, RES), HALF ** -0.5, 0.375),
        "second_filter_weight": scatter_about(key_of[4], (2, RES, GATE), (2 * RES) ** -0.5, 0.25),
        "second_residual_matrix": scatter_about(key_of[5], (HALF, RES), HALF ** -0.5, 0.375),
    }


def contract_rows(left, right):
    return lax.dot_general(left, right, (((0,), (0,)), ((), ())), preferred_element_type=jnp.float32)


def contract_cols(left, right):
    return lax.dot_general(left, right, (((1,), (1,)), ((), ())), preferred_element_type=jnp.float32)


def gate_forward(current, earlier, conv_weight):
    pre = jnp.dot(earlier, conv_weight[0], preferred_element_type=jnp.float32) + jnp.dot(current, conv_weight[1], preferred_element_type=jnp.float32)
    half_width = pre.shape[1] // 2
    gated = (jnp.tanh(pre[:, :half_width]) * jax.nn.sigmoid(pre[:, half_width:])).astype(jnp.bfloat16)
    return pre, gated


def gate_backward(current, earlier, conv_weight, out_weight, pre, gated, grad_out):
    half_width = pre.shape[1] // 2
    tanh_part = jnp.tanh(pre[:, :half_width])
    sig_part = jax.nn.sigmoid(pre[:, half_width:])
    grad_gated = contract_cols(grad_out, out_weight)
    grad_pre = jnp.concatenate([grad_gated * sig_part * (1.0 - tanh_part * tanh_part), grad_gated * tanh_part * sig_part * (1.0 - sig_part)], axis=1).astype(jnp.bfloat16)
    grad_conv = jnp.stack([contract_rows(earlier, grad_pre), contract_rows(current, grad_pre)])
    grad_proj = contract_rows(gated, grad_out)
    direct = grad_out.astype(jnp.float32) + contract_cols(grad_pre, conv_weight[1])
    return grad_conv, grad_proj, grad_pre, direct


def delayed(values, span):
    filler = jnp.zeros((values.shape[0], span, values.shape[2]), values.dtype)
    return jnp.concatenate([filler, values[:, :values.shape[1] - span]], axis=1)


def advanced(values, span):
    filler = jnp.zeros((values.shape[0], span, values.shape[2]), values.dtype)
    return jnp.concatenate([values[:, span:], filler], axis=1)


def layer_ahead_pass(current, conv_weight, out_weight, span):
    earlier = delayed(current, span)

    def per_block(pieces):
        block_in, block_past = pieces
        pre, gated = gate_forward(block_in, block_past, conv_weight)
        return (block_in.astype(jnp.float32) + jnp.dot(gated, out_weight, preferred_element_type=jnp.float32)).astype(jnp.bfloat16)

    result = lax.map(per_block, (current.reshape(-1, L_DEV, RES), earlier.reshape(-1, L_DEV, RES)))
    return result.reshape(current.shape)


def layer_reverse_pass(current, grad_out, conv_weight, out_weight, span):
    earlier = delayed(current, span)

    def per_block(totals, pieces):
        block_in, block_past, block_grad = pieces
        pre, gated = gate_forward(block_in, block_past, conv_weight)
        grad_conv, grad_proj, grad_pre, direct = gate_backward(block_in, block_past, conv_weight, out_weight, pre, gated, block_grad)
        tap_back = contract_cols(grad_pre, conv_weight[0]).astype(jnp.bfloat16)
        return (totals[0] + grad_conv, totals[1] + grad_proj), (direct, tap_back)

    start_totals = (jnp.zeros((2, RES, GATE), jnp.float32), jnp.zeros((HALF, RES), jnp.float32))
    totals, outputs = lax.scan(per_block, start_totals, (current.reshape(-1, L_DEV, RES), earlier.reshape(-1, L_DEV, RES), grad_out.reshape(-1, L_DEV, RES)))
    direct = outputs[0].reshape(current.shape)
    tap_back = outputs[1].reshape(current.shape)
    grad_in = (direct + advanced(tap_back, span).astype(jnp.float32)).astype(jnp.bfloat16)
    return grad_in, totals[0], totals[1]


def reference(inputs, cotangent, first_filter_weight, first_residual_matrix, second_filter_weight, second_residual_matrix):
    between_layers = layer_ahead_pass(inputs, first_filter_weight, first_residual_matrix, SPACING_FIRST)
    between_layers_gradient, second_filter_gradient, second_residual_gradient = layer_reverse_pass(between_layers, cotangent, second_filter_weight, second_residual_matrix, SPACING_SECOND)
    gradient_by_input, first_filter_gradient, first_residual_gradient = layer_reverse_pass(inputs, between_layers_gradient, first_filter_weight, first_residual_matrix, SPACING_FIRST)
    norm_factor = float(STREAMS * TLEN) ** -0.5
    grads_first = jnp.concatenate([first_filter_gradient.reshape(-1), first_residual_gradient.reshape(-1)]) * norm_factor
    grads_second = jnp.concatenate([second_filter_gradient.reshape(-1), second_residual_gradient.reshape(-1)]) * norm_factor
    return gradient_by_input, grads_first, grads_second
```

```python
import jax
import jax.numpy as jnp
from jax import lax
from jax.sharding import Mesh
from jax.sharding import PartitionSpec as P

CHUNKS = 1


def split_axes(mesh):
    blocks = mesh.devices.shape[1]
    member = min(32, blocks // 2)
    split = mesh.devices.reshape(mesh.devices.shape[0], blocks // member, member)
    return Mesh(split, ("dp", "group", "member"))


def from_behind(block, distance):
    devices = range(lax.axis_size("group") * lax.axis_size("member"))
    route = [(i - distance, i) for i in devices if i - distance in devices]
    return lax.ppermute(block, ("group", "member"), route)


def contract_rows(left, right):
    return lax.dot_general(
        left, right, (((0,), (0,)), ((), ())), preferred_element_type=jnp.float32
    )


def contract_cols(left, right):
    return lax.dot_general(
        left, right, (((1,), (1,)), ((), ())), preferred_element_type=jnp.float32
    )


def gates(current, earlier, conv_weight):
    pre = jnp.dot(earlier, conv_weight[0], preferred_element_type=jnp.float32) + jnp.dot(
        current, conv_weight[1], preferred_element_type=jnp.float32
    )
    half_width = pre.shape[1] // 2
    return jnp.tanh(pre[:, :half_width]), jax.nn.sigmoid(pre[:, half_width:])


def gate_gradient(tanh_part, sig_part, out_weight, grad_out):
    grad_gated = contract_cols(grad_out, out_weight)
    return jnp.concatenate(
        [
            grad_gated * sig_part * (1.0 - tanh_part * tanh_part),
            grad_gated * tanh_part * sig_part * (1.0 - sig_part),
        ],
        axis=1,
    ).astype(jnp.bfloat16)


def sum_first_stage(terms, scale):
    parts = lax.axis_size("dp") * lax.axis_size("group")
    sent = (terms * scale).astype(jnp.bfloat16).reshape(parts, lax.axis_size("member"), -1)
    received = lax.all_to_all(sent, ("dp", "group"), 0, 0, tiled=True)
    return jnp.sum(received.astype(jnp.float32), axis=0)


def per_device(x, cotangent, conv_first, proj_first, conv_second, proj_second):
    shape = x.shape
    channels = shape[2]
    rows = shape[0] * shape[1]
    blocks = lax.axis_size("group") * lax.axis_size("member")
    near = min(8, blocks // 16)
    far = min(32, blocks // 4)
    scale = float(rows * lax.axis_size("dp") * blocks) ** (-0.5)
    step = rows // CHUNKS

    def pieces(array):
        array = array.reshape(rows, -1)
        return [array[k * step : (k + 1) * step] for k in range(CHUNKS)]

    x, cot = pieces(x), pieces(cotangent)
    past = [from_behind(part, near) for part in x]
    cot_ahead = pieces(from_behind(cotangent.reshape(rows, channels), -far))
    first, middle, middle_past, middle_ahead = [], [], [], []
    for part, earlier in zip(x, past):
        t, s = gates(part, earlier, conv_first)
        gated = (t * s).astype(jnp.bfloat16)
        mid = (
            part.astype(jnp.float32)
            + jnp.dot(gated, proj_first, preferred_element_type=jnp.float32)
        ).astype(jnp.bfloat16)
        first.append((t, s, gated))
        middle.append(mid)
        middle_past.append(from_behind(mid, far))
        middle_ahead.append(from_behind(mid, -far))
    gated_second, grad_pre_first, grad_pre_second, grad_middle, direct, tap_back = (
        [],
        [],
        [],
        [],
        [],
        [],
    )
    for k in range(CHUNKS):
        t, s = gates(middle_ahead[k], middle[k], conv_second)
        ahead = gate_gradient(t, s, proj_second, cot_ahead[k])
        back = contract_cols(ahead, conv_second[0]).astype(jnp.bfloat16)
        t, s = gates(middle[k], middle_past[k], conv_second)
        gated_second.append((t * s).astype(jnp.bfloat16))
        here = gate_gradient(t, s, proj_second, cot[k])
        grad_pre_second.append(here)
        grad = (
            cot[k].astype(jnp.float32)
            + contract_cols(here, conv_second[1])
            + back.astype(jnp.float32)
        ).astype(jnp.bfloat16)
        grad_middle.append(grad)
        t, s, _ = first[k]
        here = gate_gradient(t, s, proj_first, grad)
        grad_pre_first.append(here)
        tap_back.append(
            from_behind(contract_cols(here, conv_first[0]).astype(jnp.bfloat16), -near)
        )
        direct.append(grad.astype(jnp.float32) + contract_cols(here, conv_first[1]))

    def whole(parts):
        return jnp.concatenate(parts, axis=0)

    def weight_gradient(earlier, current, grad_pre, gated, grad_out):
        grad_pre = whole(grad_pre)
        return jnp.concatenate(
            [
                contract_rows(whole(earlier), grad_pre).reshape(-1),
                contract_rows(whole(current), grad_pre).reshape(-1),
                contract_rows(whole(gated), whole(grad_out)).reshape(-1),
            ]
        )

    terms_second = weight_gradient(middle_past, middle, grad_pre_second, gated_second, cot)
    sums_second = sum_first_stage(terms_second, scale)
    terms_first = weight_gradient(past, x, grad_pre_first, [g for _, _, g in first], grad_middle)
    sums_first = sum_first_stage(terms_first, scale)
    sent = jnp.concatenate([sums_first, sums_second], axis=1).astype(jnp.bfloat16)
    received = lax.all_to_all(sent, "member", 0, 0, tiled=True)
    sums = jnp.sum(received.astype(jnp.float32), axis=0)
    length = sums.shape[0] // 2
    grad_x = whole(
        [(d + back.astype(jnp.float32)).astype(jnp.bfloat16) for d, back in zip(direct, tap_back)]
    )
    return grad_x.reshape(shape), sums[:length], sums[length:]


def solution(mesh):
    time, flat = P("dp", ("group", "member"), None), P(("dp", "group", "member"))
    return jax.shard_map(
        per_device,
        mesh=split_axes(mesh),
        in_specs=(time, time, P(), P(), P(), P()),
        out_specs=(time, flat, flat),
        check_vma=False,
    )
```

```python
import jax
import jax.numpy as jnp
from jax import lax
from jax.sharding import Mesh
from jax.sharding import PartitionSpec as P

CHUNKS = (0, 384, 768, 1024)


def split_axes(mesh):
    blocks = mesh.devices.shape[1]
    member = min(32, blocks // 2)
    split = mesh.devices.reshape(mesh.devices.shape[0], blocks // member, member)
    return Mesh(split, ("dp", "group", "member"))


def from_behind(block, distance):
    devices = range(lax.axis_size("group") * lax.axis_size("member"))
    route = [(i - distance, i) for i in devices if i - distance in devices]
    return lax.ppermute(block, ("group", "member"), route)


def contract_rows(left, right):
    return lax.dot_general(
        left, right, (((0,), (0,)), ((), ())), preferred_element_type=jnp.float32
    )


def contract_cols(left, right):
    return lax.dot_general(
        left, right, (((1,), (1,)), ((), ())), preferred_element_type=jnp.float32
    )


def gates(current, earlier, conv_weight):
    pre = jnp.dot(earlier, conv_weight[0], preferred_element_type=jnp.float32) + jnp.dot(
        current, conv_weight[1], preferred_element_type=jnp.float32
    )
    return halves(pre)


def halves(pre):
    half_width = pre.shape[1] // 2
    return jnp.tanh(pre[:, :half_width]), jax.nn.sigmoid(pre[:, half_width:])


def gate_gradient(tanh_part, sig_part, out_weight, grad_out):
    grad_gated = contract_cols(grad_out, out_weight)
    return jnp.concatenate(
        [
            grad_gated * sig_part * (1.0 - tanh_part * tanh_part),
            grad_gated * tanh_part * sig_part * (1.0 - sig_part),
        ],
        axis=1,
    ).astype(jnp.bfloat16)


def pack(terms_first, terms_second, scale):
    parts = lax.axis_size("dp") * lax.axis_size("group")
    members = lax.axis_size("member")
    return jnp.concatenate(
        [
            (terms * scale).astype(jnp.bfloat16).reshape(parts, members, -1)
            for terms in (terms_first, terms_second)
        ],
        axis=2,
    )


def per_device(x, cotangent, conv_first, proj_first, conv_second, proj_second):
    shape = x.shape
    channels = shape[2]
    rows = shape[0] * shape[1]
    blocks = lax.axis_size("group") * lax.axis_size("member")
    near = min(8, blocks // 16)
    far = min(32, blocks // 4)
    scale = float(rows * lax.axis_size("dp") * blocks) ** (-0.5)
    edges = [edge * rows // 1024 for edge in CHUNKS]
    last = len(edges) - 2

    def pieces(array):
        array = array.reshape(rows, -1)
        return [array[start:end] for start, end in zip(edges, edges[1:])]

    x, cot = pieces(x), pieces(cotangent)
    own, past = [], []
    sent = x[0]
    for k in range(last + 1):
        past.append(from_behind(sent, near))
        own.append(jnp.dot(x[k], conv_first[1], preferred_element_type=jnp.float32))
        following = x[k + 1] if k < last else cotangent
        own[k], sent = lax.optimization_barrier((own[k], following))
    cot_ahead = pieces(from_behind(sent.reshape(rows, channels), -far))
    first, middle, middle_past, middle_ahead = [], [], [], []
    for k in range(last + 1):
        if k:
            past[k], middle_past[k - 1], middle_ahead[k - 1] = lax.optimization_barrier(
                (past[k], middle_past[k - 1], middle_ahead[k - 1])
            )
        t, s = halves(
            own[k] + jnp.dot(past[k], conv_first[0], preferred_element_type=jnp.float32)
        )
        gated = (t * s).astype(jnp.bfloat16)
        mid = (
            x[k].astype(jnp.float32)
            + jnp.dot(gated, proj_first, preferred_element_type=jnp.float32)
        ).astype(jnp.bfloat16)
        first.append((t, s, gated))
        middle.append(mid)
        middle_past.append(from_behind(mid, far))
        middle_ahead.append(from_behind(mid, -far))
    direct, tap_back = [], []
    totals = None
    for k in range(last + 1):
        t, s = gates(middle_ahead[k], middle[k], conv_second)
        ahead = gate_gradient(t, s, proj_second, cot_ahead[k])
        back = contract_cols(ahead, conv_second[0]).astype(jnp.bfloat16)
        t, s = gates(middle[k], middle_past[k], conv_second)
        gated_second = (t * s).astype(jnp.bfloat16)
        grad_pre_second = gate_gradient(t, s, proj_second, cot[k])
        grad = (
            cot[k].astype(jnp.float32)
            + contract_cols(grad_pre_second, conv_second[1])
            + back.astype(jnp.float32)
        ).astype(jnp.bfloat16)
        t, s, gated = first[k]
        grad_pre = gate_gradient(t, s, proj_first, grad)
        tap = contract_cols(grad_pre, conv_first[0]).astype(jnp.bfloat16)
        tap_back.append(from_behind(tap, -near))
        direct.append(grad.astype(jnp.float32) + contract_cols(grad_pre, conv_first[1]))
        terms = [
            contract_rows(past[k], grad_pre),
            contract_rows(x[k], grad_pre),
            contract_rows(gated, grad),
            contract_rows(middle_past[k], grad_pre_second),
            contract_rows(middle[k], grad_pre_second),
            contract_rows(gated_second, cot[k]),
        ]
        totals = terms if totals is None else [a + b for a, b in zip(totals, terms)]
    totals = [total.reshape(-1) for total in totals]
    sent = pack(jnp.concatenate(totals[:3]), jnp.concatenate(totals[3:]), scale)
    early = lax.optimization_barrier((sent, *tap_back[:last]))
    tap_back[:last] = early[1:]
    received = lax.all_to_all(early[0], ("dp", "group"), 0, 0, tiled=True)
    sent = jnp.sum(received.astype(jnp.float32), axis=0).astype(jnp.bfloat16)
    received = lax.all_to_all(sent, "member", 0, 0, tiled=True)
    sums = jnp.sum(received.astype(jnp.float32), axis=0)
    length = sums.shape[0] // 2
    grad_x = jnp.concatenate(
        [(d + back.astype(jnp.float32)).astype(jnp.bfloat16) for d, back in zip(direct, tap_back)]
    )
    return grad_x.reshape(shape), sums[:length], sums[length:]


def solution(mesh):
    time, flat = P("dp", ("group", "member"), None), P(("dp", "group", "member"))
    return jax.shard_map(
        per_device,
        mesh=split_axes(mesh),
        in_specs=(time, time, P(), P(), P(), P()),
        out_specs=(time, flat, flat),
        check_vma=False,
    )
```

```python
import functools

import jax
import jax.numpy as jnp
from jax import lax
from jax.experimental import pallas as pl
from jax.experimental.pallas import tpu as pltpu
from jax.sharding import Mesh
from jax.sharding import PartitionSpec as P

SHIFT = 3
TILE = 512
BESIDE = 2 * 10**10
VMEM_LIMIT = 16 * 1024 * 1024
LANES = 128


def split_axes(mesh):
    blocks = mesh.devices.shape[1]
    member = min(32, blocks // 2)
    split = mesh.devices.reshape(mesh.devices.shape[0], blocks // member, member)
    return Mesh(split, ("dp", "group", "member"))


def move(block, route):
    return lax.ppermute(block, ("group", "member"), route)


def contract_rows(left, right):
    return lax.dot_general(
        left, right, (((0,), (0,)), ((), ())), preferred_element_type=jnp.float32
    )


def contract_cols(left, right):
    return lax.dot_general(
        left, right, (((1,), (1,)), ((), ())), preferred_element_type=jnp.float32
    )


def gates(current, earlier, conv_weight):
    pre = jnp.dot(earlier, conv_weight[0], preferred_element_type=jnp.float32) + jnp.dot(
        current, conv_weight[1], preferred_element_type=jnp.float32
    )
    return halves(pre)


def halves(pre):
    half_width = pre.shape[1] // 2
    return jnp.tanh(pre[:, :half_width]), jax.nn.sigmoid(pre[:, half_width:])


def gate_gradient(tanh_part, sig_part, grad_gated):
    return jnp.concatenate(
        [
            grad_gated * sig_part * (1.0 - tanh_part * tanh_part),
            grad_gated * tanh_part * sig_part * (1.0 - sig_part),
        ],
        axis=1,
    ).astype(jnp.bfloat16)


def tiles(rows):
    step = min(TILE, rows)
    return [pl.ds(start, step) for start in range(0, rows, step)]


def prepare_kernel(x_ref, conv_ref, own_ref):
    for part in tiles(x_ref.shape[0]):
        own_ref[part] = jnp.dot(x_ref[part], conv_ref[1], preferred_element_type=jnp.float32)


def ahead_kernel(cot_ref, proj_ref, gated_ref):
    for part in tiles(cot_ref.shape[0]):
        gated_ref[part] = contract_cols(cot_ref[part], proj_ref[...])


def forward_kernel(
    x_ref, past_ref, own_ref, conv_ref, proj_ref, middle_ref, gated_ref, tanh_ref, sig_ref
):
    for part in tiles(x_ref.shape[0]):
        t, s = halves(
            jnp.dot(past_ref[part], conv_ref[0], preferred_element_type=jnp.float32)
            + own_ref[part]
        )
        tanh_ref[part] = t
        sig_ref[part] = s
        gated = (t * s).astype(jnp.bfloat16)
        gated_ref[part] = gated
        middle_ref[part] = (
            x_ref[part].astype(jnp.float32)
            + jnp.dot(gated, proj_ref[...], preferred_element_type=jnp.float32)
        ).astype(jnp.bfloat16)


def backward_kernel(
    middle_ref,
    middle_past_ref,
    middle_ahead_ref,
    cot_ref,
    gated_ahead_ref,
    tanh_ref,
    sig_ref,
    conv_first_ref,
    proj_first_ref,
    conv_second_ref,
    proj_second_ref,
    tap_ref,
    direct_ref,
    gated_second_ref,
    pre_second_ref,
    grad_ref,
    pre_first_ref,
):
    for part in tiles(middle_ref.shape[0]):
        middle, cot = middle_ref[part], cot_ref[part]
        t, s = gates(middle_ahead_ref[part], middle, conv_second_ref)
        ahead = gate_gradient(t, s, gated_ahead_ref[part])
        back = contract_cols(ahead, conv_second_ref[0]).astype(jnp.bfloat16)
        t, s = gates(middle, middle_past_ref[part], conv_second_ref)
        gated_second_ref[part] = (t * s).astype(jnp.bfloat16)
        here = gate_gradient(t, s, contract_cols(cot, proj_second_ref[...]))
        pre_second_ref[part] = here
        grad = (
            cot.astype(jnp.float32)
            + contract_cols(here, conv_second_ref[1])
            + back.astype(jnp.float32)
        ).astype(jnp.bfloat16)
        grad_ref[part] = grad
        here = gate_gradient(
            tanh_ref[part], sig_ref[part], contract_cols(grad, proj_first_ref[...])
        )
        pre_first_ref[part] = here
        tap_ref[part] = contract_cols(here, conv_first_ref[0]).astype(jnp.bfloat16)
        direct_ref[part] = (
            grad.astype(jnp.float32) + contract_cols(here, conv_first_ref[1])
        ).astype(jnp.bfloat16)


def weights_kernel(scale, *refs):
    inputs, (sent_ref, lines, square) = refs[:-3], refs[-3:]

    def total(left, right):
        return contract_rows(left[...], right[...]) * scale

    share = sent_ref.shape[2]
    for layer in range(2):
        past, current, pre, gated, grad = inputs[layer * 5 : layer * 5 + 5]
        inner, width = past.shape[1], pre.shape[1]
        lines[:inner] = total(past, pre)
        lines[inner : 2 * inner] = total(current, pre)
        proj = total(gated, grad)
        columns = proj.shape[1]
        per_line = width // columns
        for i in range(columns // LANES):
            square[...] = proj[:, i * LANES : (i + 1) * LANES]
            for j in range(per_line):
                at = j * columns + i * LANES
                lines[2 * inner :, at : at + LANES] = square[
                    pl.ds(j, inner // per_line, stride=per_line)
                ]
        for part in range(sent_ref.shape[0]):
            sent_ref[part, layer] = lines[part * share : (part + 1) * share].astype(jnp.bfloat16)


def stage_kernel(received_ref, _, sent_ref, flat, slots):
    devices, layers, rows, width = received_ref.shape
    members, slot, _ = sent_ref.shape
    across = width // LANES
    share = rows * across // members
    slots[...] = jnp.zeros_like(slots)
    for layer in range(layers):
        total = jnp.sum(received_ref[:, layer].astype(jnp.float32), axis=0)
        for i in range(across):
            flat[pl.ds(i, rows, stride=across)] = total[:, i * LANES : (i + 1) * LANES]
        for j in range(share):
            slots[pl.ds(layer * share + j, members, stride=slot)] = flat[
                pl.ds(j, members, stride=share)
            ]
    for i in range(members):
        sent_ref[i] = slots[i * slot : (i + 1) * slot].astype(jnp.bfloat16)


def finish_kernel(received_ref, sums_ref):
    sums_ref[...] = jnp.sum(received_ref[...].astype(jnp.float32), axis=0)


def copy_kernel(from_ref, to_ref):
    to_ref[...] = from_ref[...]


def add_kernel(direct_ref, back_ref, grad_ref):
    grad_ref[...] = (
        direct_ref[...].astype(jnp.float32) + back_ref[...].astype(jnp.float32)
    ).astype(jnp.bfloat16)


def call(kernel, outs, *args, scratch=(), flops=0, after=0):
    moved = sum(a.size * a.dtype.itemsize for a in (*args, *outs))
    here = pl.BlockSpec(memory_space=pltpu.VMEM)
    waited = [pl.BlockSpec(memory_space=pl.ANY)] * after
    return pl.pallas_call(
        kernel,
        out_shape=tuple(outs),
        in_specs=[here] * (len(args) - after) + waited,
        out_specs=(here,) * len(outs),
        scratch_shapes=list(scratch),
        compiler_params=pltpu.CompilerParams(vmem_limit_bytes=VMEM_LIMIT),
        cost_estimate=pl.CostEstimate(flops=flops, bytes_accessed=moved, transcendentals=0),
    )(*args)


def per_device(x, cotangent, conv_first, proj_first, conv_second, proj_second):
    shape = x.shape
    channels, width = shape[2], conv_first.shape[2]
    rows = shape[0] * shape[1]
    parts = lax.axis_size("dp") * lax.axis_size("group")
    members = lax.axis_size("member")
    blocks = lax.axis_size("group") * members
    near = min(8, blocks // 16)
    far = min(32, blocks // 4)
    scale = float(rows * lax.axis_size("dp") * blocks) ** (-0.5)
    array, bf16, f32 = jax.ShapeDtypeStruct, jnp.bfloat16, jnp.float32

    def place(block):
        group, member = divmod(block, members)
        return group * members + (member - SHIFT) % members

    def pairs(span):
        return [(i, i + span) for i in range(blocks) if i + span in range(blocks)]

    narrow, wide = array((rows, channels), bf16), array((rows, width), bf16)
    single, double = array((rows, channels), f32), array((rows, width), f32)
    x, cot = x.reshape(rows, channels), cotangent.reshape(rows, channels)
    homes = [(i, place(i)) for i in range(blocks)]
    past = move(x, [(i, place(j)) for i, j in pairs(near)])
    x = move(x, homes)
    cot = move(cot, homes)
    cot_ahead = move(cot, [(place(i), place(j)) for i, j in pairs(-far)])
    (own,) = call(
        prepare_kernel, (double,), x, conv_first, flops=4 * rows * channels * channels
    )
    (gated_ahead,) = call(ahead_kernel, (single,), cot_ahead, proj_second, flops=BESIDE)
    middle, gated, tanh_part, sig_part = call(
        forward_kernel,
        (narrow, narrow, single, single),
        x,
        past,
        own,
        conv_first,
        proj_first,
        flops=6 * rows * channels * channels,
    )
    middle_past = move(middle, [(place(i), place(j)) for i, j in pairs(far)])
    middle_ahead = move(middle, [(place(i), place(j)) for i, j in pairs(-far)])
    tap, direct, gated_second, pre_second, grad, pre_first = call(
        backward_kernel,
        (narrow, narrow, narrow, wide, narrow, wide),
        middle,
        middle_past,
        middle_ahead,
        cot,
        gated_ahead,
        tanh_part,
        sig_part,
        conv_first,
        proj_first,
        conv_second,
        proj_second,
        flops=38 * rows * channels * channels,
    )
    tap_back = move(tap, [(place(j), i) for i, j in pairs(near)])
    direct = move(direct, [(j, i) for i, j in homes])
    weight_rows = 2 * channels + channels * channels // width
    (sent,) = call(
        functools.partial(weights_kernel, scale),
        (array((parts, 2, weight_rows // parts, width), bf16),),
        past,
        x,
        pre_first,
        gated,
        grad,
        middle_past,
        middle,
        pre_second,
        gated_second,
        cot,
        scratch=[pltpu.VMEM((weight_rows, width), f32), pltpu.VMEM((channels, LANES), f32)],
        flops=rows * channels * 20 * channels,
    )
    received = lax.all_to_all(sent, ("dp", "group"), 0, 0, tiled=True)
    share = weight_rows * width // (parts * members * LANES)
    slot = -(-2 * share // 16) * 16
    (tap_back,) = call(copy_kernel, (narrow,), tap_back, flops=BESIDE)
    (grad_x,) = call(add_kernel, (narrow,), direct, tap_back, flops=BESIDE)
    (sent,) = call(
        stage_kernel,
        (array((members, slot, LANES), bf16),),
        received,
        tap_back,
        scratch=[
            pltpu.VMEM((members * share, LANES), f32),
            pltpu.VMEM((members * slot, LANES), f32),
        ],
        after=1,
    )
    received = lax.all_to_all(sent, "member", 0, 0, tiled=True)
    (sums,) = call(finish_kernel, (array((slot, LANES), f32),), received)
    return (
        grad_x.reshape(shape),
        sums[:share].reshape(-1),
        sums[share : 2 * share].reshape(-1),
    )


def solution(mesh):
    time, flat = P("dp", ("group", "member"), None), P(("dp", "group", "member"))
    return jax.shard_map(
        per_device,
        mesh=split_axes(mesh),
        in_specs=(time, time, P(), P(), P(), P()),
        out_specs=(time, flat, flat),
        check_vma=False,
    )
```

```python
import functools

import jax
import jax.numpy as jnp
from jax import lax
from jax.experimental import pallas as pl
from jax.experimental.pallas import tpu as pltpu
from jax.sharding import Mesh
from jax.sharding import PartitionSpec as P

SHIFT = 3
TILE = 512
BESIDE = 2 * 10**10
VMEM_LIMIT = 16 * 1024 * 1024
LANES = 128


def split_axes(mesh):
    blocks = mesh.devices.shape[1]
    member = min(32, blocks // 2)
    split = mesh.devices.reshape(mesh.devices.shape[0], blocks // member, member)
    return Mesh(split, ("dp", "group", "member"))


def move(block, route):
    return lax.ppermute(block, ("group", "member"), route)


def contract_rows(left, right):
    return lax.dot_general(
        left, right, (((0,), (0,)), ((), ())), preferred_element_type=jnp.float32
    )


def contract_cols(left, right):
    return lax.dot_general(
        left, right, (((1,), (1,)), ((), ())), preferred_element_type=jnp.float32
    )


def gates(current, earlier, conv_weight):
    pre = jnp.dot(earlier, conv_weight[0], preferred_element_type=jnp.float32) + jnp.dot(
        current, conv_weight[1], preferred_element_type=jnp.float32
    )
    return halves(pre)


def halves(pre):
    half_width = pre.shape[1] // 2
    return jnp.tanh(pre[:, :half_width]), jax.nn.sigmoid(pre[:, half_width:])


def gate_gradient(tanh_part, sig_part, grad_gated):
    return jnp.concatenate(
        [
            grad_gated * sig_part * (1.0 - tanh_part * tanh_part),
            grad_gated * tanh_part * sig_part * (1.0 - sig_part),
        ],
        axis=1,
    ).astype(jnp.bfloat16)


def tiles(rows):
    step = min(TILE, rows)
    return [pl.ds(start, step) for start in range(0, rows, step)]


def prepare_kernel(x_ref, conv_ref, own_ref):
    for part in tiles(x_ref.shape[0]):
        own_ref[part] = jnp.dot(x_ref[part], conv_ref[1], preferred_element_type=jnp.float32)


def ahead_kernel(cot_ref, proj_ref, gated_ref):
    for part in tiles(cot_ref.shape[0]):
        gated_ref[part] = contract_cols(cot_ref[part], proj_ref[...])


def forward_kernel(
    x_ref, past_ref, own_ref, conv_ref, proj_ref, middle_ref, gated_ref, tanh_ref, sig_ref
):
    for part in tiles(x_ref.shape[0]):
        t, s = halves(
            jnp.dot(past_ref[part], conv_ref[0], preferred_element_type=jnp.float32)
            + own_ref[part]
        )
        tanh_ref[part] = t
        sig_ref[part] = s
        gated = (t * s).astype(jnp.bfloat16)
        gated_ref[part] = gated
        middle_ref[part] = (
            x_ref[part].astype(jnp.float32)
            + jnp.dot(gated, proj_ref[...], preferred_element_type=jnp.float32)
        ).astype(jnp.bfloat16)


def backward_kernel(
    middle_ref,
    middle_past_ref,
    middle_ahead_ref,
    cot_ref,
    gated_ahead_ref,
    tanh_ref,
    sig_ref,
    conv_first_ref,
    proj_first_ref,
    conv_second_ref,
    proj_second_ref,
    tap_ref,
    direct_ref,
    gated_second_ref,
    pre_second_ref,
    grad_ref,
    pre_first_ref,
):
    for part in tiles(middle_ref.shape[0]):
        middle, cot = middle_ref[part], cot_ref[part]
        t, s = gates(middle_ahead_ref[part], middle, conv_second_ref)
        ahead = gate_gradient(t, s, gated_ahead_ref[part])
        back = contract_cols(ahead, conv_second_ref[0]).astype(jnp.bfloat16)
        t, s = gates(middle, middle_past_ref[part], conv_second_ref)
        gated_second_ref[part] = (t * s).astype(jnp.bfloat16)
        here = gate_gradient(t, s, contract_cols(cot, proj_second_ref[...]))
        pre_second_ref[part] = here
        grad = (
            cot.astype(jnp.float32)
            + contract_cols(here, conv_second_ref[1])
            + back.astype(jnp.float32)
        ).astype(jnp.bfloat16)
        grad_ref[part] = grad
        here = gate_gradient(
            tanh_ref[part], sig_ref[part], contract_cols(grad, proj_first_ref[...])
        )
        pre_first_ref[part] = here
        tap_ref[part] = contract_cols(here, conv_first_ref[0]).astype(jnp.bfloat16)
        direct_ref[part] = (
            grad.astype(jnp.float32) + contract_cols(here, conv_first_ref[1])
        ).astype(jnp.bfloat16)


def weights_kernel(scale, *refs):
    inputs, (sent_ref, lines, square) = refs[:-3], refs[-3:]

    def total(left, right):
        return contract_rows(left[...], right[...]) * scale

    share = sent_ref.shape[2]
    for layer in range(2):
        past, current, pre, gated, grad = inputs[layer * 5 : layer * 5 + 5]
        inner, width = past.shape[1], pre.shape[1]
        lines[:inner] = total(past, pre)
        lines[inner : 2 * inner] = total(current, pre)
        proj = total(gated, grad)
        columns = proj.shape[1]
        per_line = width // columns
        for i in range(columns // LANES):
            square[...] = proj[:, i * LANES : (i + 1) * LANES]
            for j in range(per_line):
                at = j * columns + i * LANES
                lines[2 * inner :, at : at + LANES] = square[
                    pl.ds(j, inner // per_line, stride=per_line)
                ]
        for part in range(sent_ref.shape[0]):
            sent_ref[part, layer] = lines[part * share : (part + 1) * share].astype(jnp.bfloat16)


def stage_kernel(received_ref, sent_ref, flat, slots):
    devices, layers, rows, width = received_ref.shape
    members, slot, _ = sent_ref.shape
    across = width // LANES
    share = rows * across // members
    slots[...] = jnp.zeros_like(slots)
    for layer in range(layers):
        total = jnp.sum(received_ref[:, layer].astype(jnp.float32), axis=0)
        for i in range(across):
            flat[pl.ds(i, rows, stride=across)] = total[:, i * LANES : (i + 1) * LANES]
        for j in range(share):
            slots[pl.ds(layer * share + j, members, stride=slot)] = flat[
                pl.ds(j, members, stride=share)
            ]
    for i in range(members):
        sent_ref[i] = slots[i * slot : (i + 1) * slot].astype(jnp.bfloat16)


def finish_kernel(received_ref, first_ref, second_ref):
    sums = jnp.sum(received_ref[...].astype(jnp.float32), axis=0)
    share = first_ref.shape[0] // LANES
    for layer, out_ref in enumerate((first_ref, second_ref)):
        for i in range(share):
            out_ref[pl.ds(i * LANES, LANES)] = sums[layer * share + i]


def copy_kernel(*refs):
    half = len(refs) // 2
    for from_ref, to_ref in zip(refs[:half], refs[half:]):
        to_ref[...] = from_ref[...]


def add_kernel(back_ref, direct_ref, grad_ref):
    grad_ref[...] = (
        direct_ref[...].astype(jnp.float32) + back_ref[...].astype(jnp.float32)
    ).astype(jnp.bfloat16)


def call(kernel, outs, *args, scratch=(), flops=0):
    moved = sum(a.size * a.dtype.itemsize for a in (*args, *outs))
    here = pl.BlockSpec(memory_space=pltpu.VMEM)
    return pl.pallas_call(
        kernel,
        out_shape=tuple(outs),
        in_specs=[here] * len(args),
        out_specs=(here,) * len(outs),
        scratch_shapes=list(scratch),
        compiler_params=pltpu.CompilerParams(vmem_limit_bytes=VMEM_LIMIT),
        cost_estimate=pl.CostEstimate(flops=flops, bytes_accessed=moved, transcendentals=0),
    )(*args)


def per_device(x, cotangent, conv_first, proj_first, conv_second, proj_second):
    shape = x.shape
    channels, width = shape[2], conv_first.shape[2]
    rows = shape[0] * shape[1]
    parts = lax.axis_size("dp") * lax.axis_size("group")
    members = lax.axis_size("member")
    blocks = lax.axis_size("group") * members
    near = min(8, blocks // 16)
    far = min(32, blocks // 4)
    scale = float(rows * lax.axis_size("dp") * blocks) ** (-0.5)
    array, bf16, f32 = jax.ShapeDtypeStruct, jnp.bfloat16, jnp.float32

    def place(block):
        group, member = divmod(block, members)
        return group * members + (member - SHIFT) % members

    def pairs(span):
        return [(i, i + span) for i in range(blocks) if i + span in range(blocks)]

    narrow, wide = array((rows, channels), bf16), array((rows, width), bf16)
    single, double = array((rows, channels), f32), array((rows, width), f32)
    x, cot = x.reshape(rows, channels), cotangent.reshape(rows, channels)
    homes = [(i, place(i)) for i in range(blocks)]
    past = move(x, [(i, place(j)) for i, j in pairs(near)])
    x = move(x, homes)
    cot = move(cot, homes)
    cot_ahead = move(cot, [(place(i), place(j)) for i, j in pairs(-far)])
    weights = (conv_first, proj_first, conv_second, proj_second)
    conv_first, proj_first, conv_second, proj_second = call(
        copy_kernel, [array(w.shape, w.dtype) for w in weights], *weights
    )
    (own,) = call(
        prepare_kernel, (double,), x, conv_first, flops=4 * rows * channels * channels
    )
    (gated_ahead,) = call(ahead_kernel, (single,), cot_ahead, proj_second, flops=BESIDE)
    middle, gated, tanh_part, sig_part = call(
        forward_kernel,
        (narrow, narrow, single, single),
        x,
        past,
        own,
        conv_first,
        proj_first,
        flops=6 * rows * channels * channels,
    )
    middle_past = move(middle, [(place(i), place(j)) for i, j in pairs(far)])
    middle_ahead = move(middle, [(place(i), place(j)) for i, j in pairs(-far)])
    tap, direct, gated_second, pre_second, grad, pre_first = call(
        backward_kernel,
        (narrow, narrow, narrow, wide, narrow, wide),
        middle,
        middle_past,
        middle_ahead,
        cot,
        gated_ahead,
        tanh_part,
        sig_part,
        conv_first,
        proj_first,
        conv_second,
        proj_second,
        flops=38 * rows * channels * channels,
    )
    direct = move(direct, [(j, i) for i, j in homes])
    tap_back = move(tap, [(place(j), i) for i, j in pairs(near)])
    weight_rows = 2 * channels + channels * channels // width
    (sent,) = call(
        functools.partial(weights_kernel, scale),
        (array((parts, 2, weight_rows // parts, width), bf16),),
        past,
        x,
        pre_first,
        gated,
        grad,
        middle_past,
        middle,
        pre_second,
        gated_second,
        cot,
        scratch=[pltpu.VMEM((weight_rows, width), f32), pltpu.VMEM((channels, LANES), f32)],
        flops=rows * channels * 20 * channels,
    )
    received = lax.all_to_all(sent, ("dp", "group"), 0, 0, tiled=True)
    share = weight_rows * width // (parts * members * LANES)
    slot = -(-2 * share // 16) * 16
    (grad_x,) = call(add_kernel, (narrow,), tap_back, direct)
    (sent,) = call(
        stage_kernel,
        (array((members, slot, LANES), bf16),),
        received,
        scratch=[
            pltpu.VMEM((members * share, LANES), f32),
            pltpu.VMEM((members * slot, LANES), f32),
        ],
    )
    received = lax.all_to_all(sent, "member", 0, 0, tiled=True)
    own_share = array((share * LANES,), f32)
    sums_first, sums_second = call(finish_kernel, (own_share, own_share), received)
    return grad_x.reshape(shape), sums_first, sums_second


def solution(mesh):
    time, flat = P("dp", ("group", "member"), None), P(("dp", "group", "member"))
    return jax.shard_map(
        per_device,
        mesh=split_axes(mesh),
        in_specs=(time, time, P(), P(), P(), P()),
        out_specs=(time, flat, flat),
        check_vma=False,
    )
```

```python
import functools

import jax
import jax.numpy as jnp
from jax import lax
from jax.experimental import pallas as pl
from jax.experimental.pallas import tpu as pltpu
from jax.sharding import Mesh
from jax.sharding import PartitionSpec as P

SHIFT = 3
TILE = 512
BESIDE = 2 * 10**10
VMEM_LIMIT = 16 * 1024 * 1024
LANES = 128
BLOCKS = ("group", "ring", "core")


def split_axes(mesh):
    blocks = mesh.devices.shape[1]
    ring = min(16, blocks // 4)
    split = mesh.devices.reshape(mesh.devices.shape[0], blocks // (2 * ring), ring, 2)
    return Mesh(split, ("dp", *BLOCKS))


def move(block, route):
    return lax.ppermute(block, BLOCKS, route)


def contract_rows(left, right):
    return lax.dot_general(
        left, right, (((0,), (0,)), ((), ())), preferred_element_type=jnp.float32
    )


def contract_cols(left, right):
    return lax.dot_general(
        left, right, (((1,), (1,)), ((), ())), preferred_element_type=jnp.float32
    )


def gates(current, earlier, conv_weight):
    pre = jnp.dot(earlier, conv_weight[0], preferred_element_type=jnp.float32) + jnp.dot(
        current, conv_weight[1], preferred_element_type=jnp.float32
    )
    return halves(pre)


def halves(pre):
    half_width = pre.shape[1] // 2
    return jnp.tanh(pre[:, :half_width]), jax.nn.sigmoid(pre[:, half_width:])


def gate_gradient(tanh_part, sig_part, grad_gated):
    return jnp.concatenate(
        [
            grad_gated * sig_part * (1.0 - tanh_part * tanh_part),
            grad_gated * tanh_part * sig_part * (1.0 - sig_part),
        ],
        axis=1,
    ).astype(jnp.bfloat16)


def tiles(rows):
    step = min(TILE, rows)
    return [pl.ds(start, step) for start in range(0, rows, step)]


def prepare_kernel(x_ref, conv_ref, own_ref):
    for part in tiles(x_ref.shape[0]):
        own_ref[part] = jnp.dot(x_ref[part], conv_ref[1], preferred_element_type=jnp.float32)


def ahead_kernel(cot_ref, proj_ref, gated_ref):
    for part in tiles(cot_ref.shape[0]):
        gated_ref[part] = contract_cols(cot_ref[part], proj_ref[...])


def forward_kernel(
    x_ref, past_ref, own_ref, conv_ref, proj_ref, middle_ref, gated_ref, tanh_ref, sig_ref
):
    for part in tiles(x_ref.shape[0]):
        t, s = halves(
            jnp.dot(past_ref[part], conv_ref[0], preferred_element_type=jnp.float32)
            + own_ref[part]
        )
        tanh_ref[part] = t
        sig_ref[part] = s
        gated = (t * s).astype(jnp.bfloat16)
        gated_ref[part] = gated
        middle_ref[part] = (
            x_ref[part].astype(jnp.float32)
            + jnp.dot(gated, proj_ref[...], preferred_element_type=jnp.float32)
        ).astype(jnp.bfloat16)


def tap_kernel(middle_ref, middle_ahead_ref, gated_ahead_ref, conv_ref, tap_ref):
    for part in tiles(middle_ref.shape[0]):
        t, s = gates(middle_ahead_ref[part], middle_ref[part], conv_ref)
        ahead = gate_gradient(t, s, gated_ahead_ref[part])
        tap_ref[part] = contract_cols(ahead, conv_ref[0]).astype(jnp.bfloat16)


def backward_kernel(
    middle_ref,
    middle_past_ref,
    tap_second_ref,
    cot_ref,
    tanh_ref,
    sig_ref,
    conv_first_ref,
    proj_first_ref,
    conv_second_ref,
    proj_second_ref,
    tap_ref,
    direct_ref,
    gated_second_ref,
    pre_second_ref,
    grad_ref,
    pre_first_ref,
):
    for part in tiles(middle_ref.shape[0]):
        middle, cot = middle_ref[part], cot_ref[part]
        t, s = gates(middle, middle_past_ref[part], conv_second_ref)
        gated_second_ref[part] = (t * s).astype(jnp.bfloat16)
        here = gate_gradient(t, s, contract_cols(cot, proj_second_ref[...]))
        pre_second_ref[part] = here
        grad = (
            cot.astype(jnp.float32)
            + contract_cols(here, conv_second_ref[1])
            + tap_second_ref[part].astype(jnp.float32)
        ).astype(jnp.bfloat16)
        grad_ref[part] = grad
        here = gate_gradient(
            tanh_ref[part], sig_ref[part], contract_cols(grad, proj_first_ref[...])
        )
        pre_first_ref[part] = here
        tap_ref[part] = contract_cols(here, conv_first_ref[0]).astype(jnp.bfloat16)
        direct_ref[part] = (
            grad.astype(jnp.float32) + contract_cols(here, conv_first_ref[1])
        ).astype(jnp.bfloat16)


def weights_kernel(scale, ring, *refs):
    inputs, (sent_ref, flat) = refs[:-2], refs[-2:]
    devices, _, rows, _ = sent_ref.shape
    share = rows // ring

    def put(start, left, right):
        total = contract_rows(left[...], right[...]) * scale
        inner, across = total.shape[0], total.shape[1] // LANES
        for i in range(across):
            flat[pl.ds(start + i, inner, stride=across)] = total[:, i * LANES : (i + 1) * LANES]
        return start + inner * across

    for layer in range(2):
        past, current, pre, gated, grad = inputs[layer * 5 : layer * 5 + 5]
        put(put(put(0, past, pre), current, pre), gated, grad)
        for device in range(devices):
            group, core = divmod(device, 2)
            for j in range(share):
                start = (group * ring * 2 + core) * share + j
                sent_ref[device, layer, j * ring : (j + 1) * ring] = flat[
                    pl.ds(start, ring, stride=2 * share)
                ].astype(jnp.bfloat16)


def stage_kernel(received_ref, sent_ref, slots):
    _, layers, rows, _ = received_ref.shape
    ring, slot, _ = sent_ref.shape
    share = rows // ring
    slots[...] = jnp.zeros_like(slots)
    for layer in range(layers):
        total = jnp.sum(received_ref[:, layer].astype(jnp.float32), axis=0)
        for j in range(share):
            slots[pl.ds(layer * share + j, ring, stride=slot)] = total[j * ring : (j + 1) * ring]
    for i in range(ring):
        sent_ref[i] = slots[i * slot : (i + 1) * slot].astype(jnp.bfloat16)


def finish_kernel(received_ref, first_ref, second_ref):
    sums = jnp.sum(received_ref[...].astype(jnp.float32), axis=0)
    share = first_ref.shape[0] // LANES
    for layer, out_ref in enumerate((first_ref, second_ref)):
        for i in range(share):
            out_ref[pl.ds(i * LANES, LANES)] = sums[layer * share + i]


def copy_kernel(*refs):
    half = len(refs) // 2
    for from_ref, to_ref in zip(refs[:half], refs[half:]):
        to_ref[...] = from_ref[...]


def add_kernel(back_ref, direct_ref, grad_ref):
    grad_ref[...] = (
        direct_ref[...].astype(jnp.float32) + back_ref[...].astype(jnp.float32)
    ).astype(jnp.bfloat16)


def call(kernel, outs, *args, scratch=(), flops=0):
    moved = sum(a.size * a.dtype.itemsize for a in (*args, *outs))
    here = pl.BlockSpec(memory_space=pltpu.VMEM)
    return pl.pallas_call(
        kernel,
        out_shape=tuple(outs),
        in_specs=[here] * len(args),
        out_specs=(here,) * len(outs),
        scratch_shapes=list(scratch),
        compiler_params=pltpu.CompilerParams(vmem_limit_bytes=VMEM_LIMIT),
        cost_estimate=pl.CostEstimate(flops=flops, bytes_accessed=moved, transcendentals=0),
    )(*args)


def per_device(x, cotangent, conv_first, proj_first, conv_second, proj_second):
    shape = x.shape
    channels, width = shape[2], conv_first.shape[2]
    rows = shape[0] * shape[1]
    ring = lax.axis_size("ring")
    members = 2 * ring
    blocks = lax.axis_size("group") * members
    plane = lax.axis_size("dp") * lax.axis_size("group") * 2
    near = min(8, blocks // 16)
    far = min(32, blocks // 4)
    scale = float(rows * lax.axis_size("dp") * blocks) ** (-0.5)
    array, bf16, f32 = jax.ShapeDtypeStruct, jnp.bfloat16, jnp.float32

    def place(block):
        group, member = divmod(block, members)
        return group * members + (member - SHIFT) % members

    def pairs(span):
        return [(i, i + span) for i in range(blocks) if i + span in range(blocks)]

    narrow, wide = array((rows, channels), bf16), array((rows, width), bf16)
    single, double = array((rows, channels), f32), array((rows, width), f32)
    x, cot = x.reshape(rows, channels), cotangent.reshape(rows, channels)
    homes = [(i, place(i)) for i in range(blocks)]
    past = move(x, [(i, place(j)) for i, j in pairs(near)])
    x = move(x, homes)
    cot = move(cot, homes)
    cot_ahead = move(cot, [(place(i), place(j)) for i, j in pairs(-far)])
    weights = (conv_first, proj_first, conv_second, proj_second)
    conv_first, proj_first, conv_second, proj_second = call(
        copy_kernel, [array(w.shape, w.dtype) for w in weights], *weights
    )
    (own,) = call(
        prepare_kernel, (double,), x, conv_first, flops=4 * rows * channels * channels
    )
    (gated_ahead,) = call(ahead_kernel, (single,), cot_ahead, proj_second, flops=BESIDE)
    middle, gated, tanh_part, sig_part = call(
        forward_kernel,
        (narrow, narrow, single, single),
        x,
        past,
        own,
        conv_first,
        proj_first,
        flops=6 * rows * channels * channels,
    )
    middle_past = move(middle, [(place(i), place(j)) for i, j in pairs(far)])
    middle_ahead = move(middle, [(place(i), place(j)) for i, j in pairs(-far)])
    (tap_second,) = call(
        tap_kernel,
        (narrow,),
        middle,
        middle_ahead,
        gated_ahead,
        conv_second,
        flops=12 * rows * channels * channels,
    )
    tap, direct, gated_second, pre_second, grad, pre_first = call(
        backward_kernel,
        (narrow, narrow, narrow, wide, narrow, wide),
        middle,
        middle_past,
        tap_second,
        cot,
        tanh_part,
        sig_part,
        conv_first,
        proj_first,
        conv_second,
        proj_second,
        flops=26 * rows * channels * channels,
    )
    direct = move(direct, [(j, i) for i, j in homes])
    tap_back = move(tap, [(place(j), i) for i, j in pairs(near)])
    units = (2 * channels * width + channels * channels) // LANES
    share = units // (plane * ring)
    (sent,) = call(
        functools.partial(weights_kernel, scale, ring),
        (array((plane, 2, ring * share, LANES), bf16),),
        past,
        x,
        pre_first,
        gated,
        grad,
        middle_past,
        middle,
        pre_second,
        gated_second,
        cot,
        scratch=[pltpu.VMEM((units, LANES), f32)],
        flops=rows * channels * 20 * channels,
    )
    received = lax.all_to_all(sent, ("dp", "group", "core"), 0, 0, tiled=True)
    slot = -(-2 * share // 16) * 16
    (sent,) = call(
        stage_kernel,
        (array((ring, slot, LANES), bf16),),
        received,
        scratch=[pltpu.VMEM((ring * slot, LANES), f32)],
    )
    received = lax.all_to_all(sent, "ring", 0, 0, tiled=True)
    (grad_x,) = call(add_kernel, (narrow,), tap_back, direct)
    own_share = array((share * LANES,), f32)
    sums_first, sums_second = call(finish_kernel, (own_share, own_share), received)
    return grad_x.reshape(shape), sums_first, sums_second


def solution(mesh):
    time, flat = P("dp", BLOCKS, None), P(("dp", *BLOCKS))
    return jax.shard_map(
        per_device,
        mesh=split_axes(mesh),
        in_specs=(time, time, P(), P(), P(), P()),
        out_specs=(time, flat, flat),
        check_vma=False,
    )
```

```python
import functools

import jax
import jax.numpy as jnp
from jax import lax
from jax.experimental import pallas as pl
from jax.experimental.pallas import tpu as pltpu
from jax.sharding import Mesh
from jax.sharding import PartitionSpec as P

SHIFT = 3
TILE = 512
BESIDE = 2 * 10**10
VMEM_LIMIT = 16 * 1024 * 1024
LANES = 128
BLOCKS = ("group", "ring", "core")


def split_axes(mesh):
    blocks = mesh.devices.shape[1]
    ring = min(16, blocks // 4)
    split = mesh.devices.reshape(mesh.devices.shape[0], blocks // (2 * ring), ring, 2)
    return Mesh(split, ("dp", *BLOCKS))


def move(block, route):
    return lax.ppermute(block, BLOCKS, route)


def contract_rows(left, right):
    return lax.dot_general(
        left, right, (((0,), (0,)), ((), ())), preferred_element_type=jnp.float32
    )


def contract_cols(left, right):
    return lax.dot_general(
        left, right, (((1,), (1,)), ((), ())), preferred_element_type=jnp.float32
    )


def gates(current, earlier, conv_weight):
    pre = jnp.dot(earlier, conv_weight[0], preferred_element_type=jnp.float32) + jnp.dot(
        current, conv_weight[1], preferred_element_type=jnp.float32
    )
    return halves(pre)


def halves(pre):
    half_width = pre.shape[1] // 2
    return jnp.tanh(pre[:, :half_width]), jax.nn.sigmoid(pre[:, half_width:])


def gate_gradient(tanh_part, sig_part, grad_gated):
    return jnp.concatenate(
        [
            grad_gated * sig_part * (1.0 - tanh_part * tanh_part),
            grad_gated * tanh_part * sig_part * (1.0 - sig_part),
        ],
        axis=1,
    ).astype(jnp.bfloat16)


def tiles(rows):
    step = min(TILE, rows)
    return [pl.ds(start, step) for start in range(0, rows, step)]


def prepare_kernel(x_ref, conv_ref, own_ref):
    for part in tiles(x_ref.shape[0]):
        own_ref[part] = jnp.dot(x_ref[part], conv_ref[1], preferred_element_type=jnp.float32)


def ahead_kernel(cot_ref, proj_ref, gated_ref):
    for part in tiles(cot_ref.shape[0]):
        gated_ref[part] = contract_cols(cot_ref[part], proj_ref[...])


def forward_kernel(
    x_ref, past_ref, own_ref, conv_ref, proj_ref, middle_ref, gated_ref, tanh_ref, sig_ref
):
    for part in tiles(x_ref.shape[0]):
        t, s = halves(
            jnp.dot(past_ref[part], conv_ref[0], preferred_element_type=jnp.float32)
            + own_ref[part]
        )
        tanh_ref[part] = t
        sig_ref[part] = s
        gated = (t * s).astype(jnp.bfloat16)
        gated_ref[part] = gated
        middle_ref[part] = (
            x_ref[part].astype(jnp.float32)
            + jnp.dot(gated, proj_ref[...], preferred_element_type=jnp.float32)
        ).astype(jnp.bfloat16)


def tap_kernel(
    odd_ref, middle_ref, even_ref, uneven_ref, gated_ahead_ref, conv_ref, tap_ref, past_ref
):
    odd = odd_ref[0] == 1
    for part in tiles(middle_ref.shape[0]):
        first, second = even_ref[part].astype(jnp.float32), uneven_ref[part].astype(jnp.float32)
        past_ref[part] = jnp.where(odd, first, second).astype(jnp.bfloat16)
        middle_ahead = jnp.where(odd, second, first).astype(jnp.bfloat16)
        t, s = gates(middle_ahead, middle_ref[part], conv_ref)
        ahead = gate_gradient(t, s, gated_ahead_ref[part])
        tap_ref[part] = contract_cols(ahead, conv_ref[0]).astype(jnp.bfloat16)


def backward_kernel(
    middle_ref,
    middle_past_ref,
    tap_second_ref,
    cot_ref,
    tanh_ref,
    sig_ref,
    conv_first_ref,
    proj_first_ref,
    conv_second_ref,
    proj_second_ref,
    tap_ref,
    direct_ref,
    gated_second_ref,
    pre_second_ref,
    grad_ref,
    pre_first_ref,
):
    for part in tiles(middle_ref.shape[0]):
        middle, cot = middle_ref[part], cot_ref[part]
        t, s = gates(middle, middle_past_ref[part], conv_second_ref)
        gated_second_ref[part] = (t * s).astype(jnp.bfloat16)
        here = gate_gradient(t, s, contract_cols(cot, proj_second_ref[...]))
        pre_second_ref[part] = here
        grad = (
            cot.astype(jnp.float32)
            + contract_cols(here, conv_second_ref[1])
            + tap_second_ref[part].astype(jnp.float32)
        ).astype(jnp.bfloat16)
        grad_ref[part] = grad
        here = gate_gradient(
            tanh_ref[part], sig_ref[part], contract_cols(grad, proj_first_ref[...])
        )
        pre_first_ref[part] = here
        tap_ref[part] = contract_cols(here, conv_first_ref[0]).astype(jnp.bfloat16)
        direct_ref[part] = (
            grad.astype(jnp.float32) + contract_cols(here, conv_first_ref[1])
        ).astype(jnp.bfloat16)


def weights_kernel(scale, ring, *refs):
    inputs, (sent_ref, flat) = refs[:-2], refs[-2:]
    devices, _, rows, _ = sent_ref.shape
    share = rows // ring

    def put(start, left, right):
        total = contract_rows(left[...], right[...]) * scale
        inner, across = total.shape[0], total.shape[1] // LANES
        for i in range(across):
            flat[pl.ds(start + i, inner, stride=across)] = total[:, i * LANES : (i + 1) * LANES]
        return start + inner * across

    for layer in range(2):
        past, current, pre, gated, grad = inputs[layer * 5 : layer * 5 + 5]
        put(put(put(0, past, pre), current, pre), gated, grad)
        for device in range(devices):
            group, core = divmod(device, 2)
            for j in range(share):
                start = (group * ring * 2 + core) * share + j
                sent_ref[device, layer, j * ring : (j + 1) * ring] = flat[
                    pl.ds(start, ring, stride=2 * share)
                ].astype(jnp.bfloat16)


def stage_kernel(received_ref, sent_ref, slots):
    _, layers, rows, _ = received_ref.shape
    ring, slot, _ = sent_ref.shape
    share = rows // ring
    slots[...] = jnp.zeros_like(slots)
    for layer in range(layers):
        total = jnp.sum(received_ref[:, layer].astype(jnp.float32), axis=0)
        for j in range(share):
            slots[pl.ds(layer * share + j, ring, stride=slot)] = total[j * ring : (j + 1) * ring]
    for i in range(ring):
        sent_ref[i] = slots[i * slot : (i + 1) * slot].astype(jnp.bfloat16)


def finish_kernel(received_ref, first_ref, second_ref):
    sums = jnp.sum(received_ref[...].astype(jnp.float32), axis=0)
    share = first_ref.shape[0] // LANES
    for layer, out_ref in enumerate((first_ref, second_ref)):
        for i in range(share):
            out_ref[pl.ds(i * LANES, LANES)] = sums[layer * share + i]


def copy_kernel(*refs):
    half = len(refs) // 2
    for from_ref, to_ref in zip(refs[:half], refs[half:]):
        to_ref[...] = from_ref[...]


def add_kernel(back_ref, direct_ref, grad_ref):
    grad_ref[...] = (
        direct_ref[...].astype(jnp.float32) + back_ref[...].astype(jnp.float32)
    ).astype(jnp.bfloat16)


def call(kernel, outs, *args, scratch=(), flops=0):
    moved = sum(a.size * a.dtype.itemsize for a in (*args, *outs))
    here = pl.BlockSpec(memory_space=pltpu.VMEM)
    scalar = pl.BlockSpec(memory_space=pltpu.SMEM)
    return pl.pallas_call(
        kernel,
        out_shape=tuple(outs),
        in_specs=[scalar if a.dtype == jnp.int32 else here for a in args],
        out_specs=(here,) * len(outs),
        scratch_shapes=list(scratch),
        compiler_params=pltpu.CompilerParams(vmem_limit_bytes=VMEM_LIMIT),
        cost_estimate=pl.CostEstimate(flops=flops, bytes_accessed=moved, transcendentals=0),
    )(*args)


def per_device(x, cotangent, conv_first, proj_first, conv_second, proj_second):
    shape = x.shape
    channels, width = shape[2], conv_first.shape[2]
    rows = shape[0] * shape[1]
    ring = lax.axis_size("ring")
    members = 2 * ring
    blocks = lax.axis_size("group") * members
    plane = lax.axis_size("dp") * lax.axis_size("group") * 2
    near = min(8, blocks // 16)
    far = min(32, blocks // 4)
    scale = float(rows * lax.axis_size("dp") * blocks) ** (-0.5)
    array, bf16, f32 = jax.ShapeDtypeStruct, jnp.bfloat16, jnp.float32

    def place(block):
        group, member = divmod(block, members)
        return group * members + (member - SHIFT) % members

    def pairs(span):
        return [(i, i + span) for i in range(blocks) if i + span in range(blocks)]

    narrow, wide = array((rows, channels), bf16), array((rows, width), bf16)
    single, double = array((rows, channels), f32), array((rows, width), f32)
    x, cot = x.reshape(rows, channels), cotangent.reshape(rows, channels)
    homes = [(i, place(i)) for i in range(blocks)]
    own_x = move(x, homes)
    past = move(x, [(i, place(j)) for i, j in pairs(near)])
    x = own_x
    cot = move(cot, homes)
    cot_ahead = move(cot, [(place(i), place(j)) for i, j in pairs(-far)])
    weights = (conv_first, proj_first, conv_second, proj_second)
    conv_first, proj_first, conv_second, proj_second = call(
        copy_kernel, [array(w.shape, w.dtype) for w in weights], *weights
    )
    (own,) = call(
        prepare_kernel, (double,), x, conv_first, flops=4 * rows * channels * channels
    )
    (gated_ahead,) = call(ahead_kernel, (single,), cot_ahead, proj_second, flops=BESIDE)
    middle, gated, tanh_part, sig_part = call(
        forward_kernel,
        (narrow, narrow, single, single),
        x,
        past,
        own,
        conv_first,
        proj_first,
        flops=6 * rows * channels * channels,
    )
    swapped = []
    for odd in range(2):
        route = [
            (place(i), place(j)) for i, j in pairs(far) + pairs(-far) if min(i, j) // far % 2 == odd
        ]
        swapped.append(move(middle, route))
    device = lax.axis_index(BLOCKS)
    block = device // members * members + (device + SHIFT) % members
    odd = (block // far % 2).astype(jnp.int32).reshape(1)
    tap_second, middle_past = call(
        tap_kernel,
        (narrow, narrow),
        odd,
        middle,
        *swapped,
        gated_ahead,
        conv_second,
        flops=12 * rows * channels * channels,
    )
    tap, direct, gated_second, pre_second, grad, pre_first = call(
        backward_kernel,
        (narrow, narrow, narrow, wide, narrow, wide),
        middle,
        middle_past,
        tap_second,
        cot,
        tanh_part,
        sig_part,
        conv_first,
        proj_first,
        conv_second,
        proj_second,
        flops=26 * rows * channels * channels,
    )
    direct = move(direct, [(j, i) for i, j in homes])
    tap_back = move(tap, [(place(j), i) for i, j in pairs(near)])
    units = (2 * channels * width + channels * channels) // LANES
    share = units // (plane * ring)
    (sent,) = call(
        functools.partial(weights_kernel, scale, ring),
        (array((plane, 2, ring * share, LANES), bf16),),
        past,
        x,
        pre_first,
        gated,
        grad,
        middle_past,
        middle,
        pre_second,
        gated_second,
        cot,
        scratch=[pltpu.VMEM((units, LANES), f32)],
        flops=rows * channels * 20 * channels,
    )
    received = lax.all_to_all(sent, ("dp", "group", "core"), 0, 0, tiled=True)
    slot = -(-2 * share // 16) * 16
    (sent,) = call(
        stage_kernel,
        (array((ring, slot, LANES), bf16),),
        received,
        scratch=[pltpu.VMEM((ring * slot, LANES), f32)],
    )
    received = lax.all_to_all(sent, "ring", 0, 0, tiled=True)
    (grad_x,) = call(add_kernel, (narrow,), tap_back, direct)
    own_share = array((share * LANES,), f32)
    sums_first, sums_second = call(finish_kernel, (own_share, own_share), received)
    return grad_x.reshape(shape), sums_first, sums_second


def solution(mesh):
    time, flat = P("dp", BLOCKS, None), P(("dp", *BLOCKS))
    return jax.shard_map(
        per_device,
        mesh=split_axes(mesh),
        in_specs=(time, time, P(), P(), P(), P()),
        out_specs=(time, flat, flat),
        check_vma=False,
    )
```
